32 devices in a mesh: track: 4 (over x, core), tm: 8 (over z, y).
Axes of the slice: x: 2, y: 2, z: 4, core: 2. Of those that a mesh axis runs over, the one named last changes fastest.
Arguments:
- diffusion_latents: bfloat16 [8, 512, 64], P(None, 'tm', 'track'), may hold values from -6 to 6
- lengths: int32 [8], P('track'), may hold values from 64 to 512, as said below
- input_conv_weight: bfloat16 [7, 64, 1024], replicated, may hold values from -0.25 to 0.25
- upsample_snake_params: float32 [2, 1024], replicated, may hold values from 0.5 to 2
- transposed_conv_weight: bfloat16 [1024, 16, 512], replicated, may hold values from -0.125 to 0.125
- residual_snake_params: float32 [2, 2, 2, 512], replicated, may hold values from 0.5 to 2
- residual_dilated_weight: bfloat16 [2, 7, 512, 512], replicated, may hold values from -0.09375 to 0.09375
- residual_pointwise_weight: bfloat16 [2, 512, 512], replicated, may hold values from -0.25 to 0.25
Outputs:
- decoded: bfloat16 [8, 4096, 512], P('track', 'tm')
The draws below stay inside these ranges and needn't reach their ends.
Inputs may be any that keep to these rules, and one draw needn't show every extreme that they name: `lengths`: every draw has at least one track of all 512 frames.
All inputs are finite; a program needn't handle non-finite values.
Results may differ from the reference program's by a relative error of at most 0.03.
Values may be sent and summed in bfloat16 or wider, within the bound.
A program may use at most 128 MiB of HBM per device.

```python
import math
import jax
import jax.numpy as jnp
from jax import lax

LATENT_CHANNELS = 64
WIDE = 1024
NARROW = 512
KERNEL = 7
STRIDE = 8
UNITS = 2
TRACK_TOTAL = 8
LATENT_FRAMES = 512


def draw_lengths(key, part):
    picker, chooser = jax.random.split(key)
    spread = jax.random.randint(picker, (TRACK_TOTAL,), LATENT_FRAMES // 8, LATENT_FRAMES + 1)
    chosen = jax.random.randint(chooser, (), 0, TRACK_TOTAL)
    return jnp.where(jnp.arange(TRACK_TOTAL) == chosen, LATENT_FRAMES, spread).astype(jnp.int32)


def level_of(rng, dims, shards, smallest, top_value):
    loudness = 1.0
    for dim, parts in shards:
        draws = jax.random.uniform(jax.random.fold_in(jax.random.fold_in(rng, 6), dim), (parts,), jnp.float32, smallest / len(shards), top_value / len(shards))
        loudness = loudness * jnp.repeat(jnp.exp(draws), dims[dim] // parts).reshape((-1,) + (1,) * (len(dims) - 1 - dim))
    return loudness


def normal_values(own_key, dims, scale, most, cuts=(), held_as=jnp.bfloat16):
    values = jax.random.normal(own_key, dims, jnp.float32) * scale
    if len(cuts) > 0:
        values = level_of(own_key, dims, cuts, -0.22, 0.18) * values
    return jnp.clip(values, min=-most, max=most).astype(held_as)


def setup_inputs(seed: int = 0) -> dict:
    key_list = jax.random.split(jax.random.key(seed), 9)
    return {
        "diffusion_latents": normal_values(key_list[0], (TRACK_TOTAL, LATENT_FRAMES, LATENT_CHANNELS), 1.0, 6.0, ((1, 8), (2, 4))),
        "lengths": draw_lengths(jax.random.fold_in(key_list[8], 71), 0),
        "input_conv_weight": normal_values(key_list[2], (KERNEL, LATENT_CHANNELS, WIDE), (KERNEL * LATENT_CHANNELS) ** -0.5, 0.25),
        "upsample_snake_params": jnp.clip(jnp.exp(jax.random.uniform(key_list[3], (2, WIDE), jnp.float32, math.log(0.5), math.log(2.0))), 0.5, 2.0),
        "transposed_conv_weight": normal_values(key_list[4], (WIDE, 2 * STRIDE, NARROW), (2 * WIDE) ** -0.5, 0.125),
        "residual_snake_params": jnp.clip(jnp.exp(jax.random.uniform(key_list[5], (UNITS, 2, 2, NARROW), jnp.float32, math.log(0.5), math.log(2.0))), 0.5, 2.0),
        "residual_dilated_weight": normal_values(key_list[6], (UNITS, KERNEL, NARROW, NARROW), (KERNEL * NARROW) ** -0.5, 0.09375),
        "residual_pointwise_weight": normal_values(key_list[7], (UNITS, NARROW, NARROW), NARROW ** -0.5, 0.25),
    }


def snake_apply(values, params):
    widened = values.astype(jnp.float32)
    return widened + jnp.sin(params[0] * widened) ** 2 / params[1]


def kernel_conv(padded, weight, spacing):
    tap_count = weight.shape[0]
    extent = padded.shape[0] - (tap_count - 1) * spacing
    summed = jnp.zeros((extent, weight.shape[2]), jnp.float32)
    for position in range(tap_count):
        window = lax.slice_in_dim(padded, position * spacing, position * spacing + extent, axis=0)
        summed = summed + jnp.dot(window, weight[position], preferred_element_type=jnp.float32)
    return summed


def reference(diffusion_latents, lengths, input_conv_weight, upsample_snake_params, transposed_conv_weight, residual_snake_params, residual_dilated_weight, residual_pointwise_weight):
    half_kernel = (input_conv_weight.shape[0] - 1) // 2
    stride = transposed_conv_weight.shape[1] // 2
    half_stride = stride // 2
    outputs = transposed_conv_weight.shape[2]

    def single_track(inputs):
        latent, length = inputs
        frame_count = latent.shape[0]
        frame_live = jnp.arange(frame_count, dtype=jnp.int32)[:, None] < length
        latent = jnp.where(frame_live, latent, jnp.zeros_like(latent))
        padded = jnp.pad(latent, ((half_kernel, half_kernel), (0, 0)))
        hidden = kernel_conv(padded, input_conv_weight, 1)
        hidden = jnp.where(frame_live, hidden, jnp.float32(0.0)).astype(jnp.bfloat16)
        shaped = snake_apply(hidden, upsample_snake_params).astype(jnp.bfloat16)
        padded = jnp.pad(shaped, ((1, 1), (0, 0)))
        flattened = transposed_conv_weight.reshape(transposed_conv_weight.shape[0], 2 * stride * outputs)
        phases = jnp.dot(padded, flattened, preferred_element_type=jnp.float32)
        phases = phases.reshape(frame_count + 2, 2 * stride, outputs)
        lower_half = phases[1:-1, half_stride:stride] + phases[:-2, stride + half_stride:]
        upper_half = phases[2:, :half_stride] + phases[1:-1, stride:stride + half_stride]
        signal = jnp.concatenate([lower_half, upper_half], axis=1).reshape(frame_count * stride, outputs)
        sample_live = jnp.arange(frame_count * stride, dtype=jnp.int32)[:, None] < length * stride
        signal = jnp.where(sample_live, signal, jnp.float32(0.0)).astype(jnp.bfloat16)
        for unit_index in range(residual_dilated_weight.shape[0]):
            spacing = 3 ** unit_index
            activated = snake_apply(signal, residual_snake_params[unit_index, 0]).astype(jnp.bfloat16)
            padded = jnp.pad(activated, ((half_kernel * spacing, half_kernel * spacing), (0, 0)))
            dilated = kernel_conv(padded, residual_dilated_weight[unit_index], spacing)
            pointed = snake_apply(dilated, residual_snake_params[unit_index, 1]).astype(jnp.bfloat16)
            branch = jnp.dot(pointed, residual_pointwise_weight[unit_index], preferred_element_type=jnp.float32)
            summed = signal.astype(jnp.float32) + branch
            signal = jnp.where(sample_live, summed, jnp.float32(0.0)).astype(jnp.bfloat16)
        return signal

    return lax.map(single_track, (diffusion_latents, lengths))
```

```python
import functools
import math

import jax
import jax.numpy as jnp
from jax import lax
from jax.experimental import pallas as pl
from jax.experimental.pallas import tpu as pltpu
from jax.sharding import PartitionSpec as P

MESH = pl.DeviceIdType.MESH
LEAD = 4
CHUNK = 64
GROUP = 2
SIN2 = (9.86952174, -32.4650355, 42.6422709, -29.4210797, 10.573119)


def snake(value, turn, gain):
    turns = value * turn
    rest = turns - jnp.round(turns)
    square = rest * rest
    wave = SIN2[-1]
    for factor in SIN2[-2::-1]:
        wave = wave * square + factor
    return value + (wave * square) * gain


def live_rows(row, per_track, base, lead, lens):
    second = row >= per_track
    frame = base - lead + row - jnp.where(second, per_track, 0)
    limit = jnp.where(second, lens[1], lens[0])
    return (frame >= 0) & (frame < limit)


def kernel(
    track_count,
    time_count,
    lens_ref,
    x_ref,
    up_ref,
    res_ref,
    wi_hbm,
    wt_hbm,
    wd_hbm,
    wp_hbm,
    out_ref,
    recv,
    wi,
    raw,
    table,
    wd,
    wp,
    columns,
    shaped,
    sig0,
    sig1,
    act0,
    act1,
    final,
    send_sem,
    recv_sem,
    own_sem,
    wi_sem,
    raw_sem,
    wd_sem,
    wp_sem,
):
    frames = x_ref.shape[2]
    rows = shaped.shape[1]
    per_track = rows // 2
    stride = sig0.shape[0]
    half = stride // 2
    width = sig0.shape[2]
    wide = table.shape[1] // 2
    part = x_ref.shape[1]
    taps = wd.shape[1]
    t = lax.axis_index("track")
    m = lax.axis_index("tm")
    base = m * frames

    chunks = raw.shape[0]
    wi_copy = pltpu.make_async_copy(wi_hbm, wi.at[pl.ds(0, wi_hbm.shape[0])], wi_sem)
    wi_copy.start()
    raw_copies = [
        pltpu.make_async_copy(wt_hbm.at[pl.ds(i * CHUNK, CHUNK)], raw.at[i], raw_sem.at[i])
        for i in range(chunks)
    ]
    for copy in raw_copies:
        copy.start()
    wd_copies = [pltpu.make_async_copy(wd_hbm.at[u], wd.at[u], wd_sem.at[u]) for u in range(2)]
    wp_copy = pltpu.make_async_copy(wp_hbm, wp, wp_sem)
    wd_copies[0].start()
    wp_copy.start()
    wd_copies[1].start()

    peers = []
    for o in range(3):
        for i in range(track_count):
            if o == 1 and i == 0:
                continue
            peers.append((o, i))
    barrier = pltpu.get_barrier_semaphore()

    def place(o, i):
        return {
            "track": lax.rem(t + i, track_count),
            "tm": lax.rem(m + o - 1 + time_count, time_count),
        }

    for o, i in peers:
        pl.semaphore_signal(barrier, inc=1, device_id=place(o, i), device_id_type=MESH)
    pl.semaphore_wait(barrier, len(peers))
    own = pltpu.make_async_copy(x_ref.at[pl.ds(2 * t, 2)], recv.at[1, t], own_sem)
    own.start()
    sends = []
    for o, i in peers:
        target = place(o, i)
        copy = pltpu.make_async_remote_copy(
            src_ref=x_ref.at[pl.ds(2 * target["track"], 2)],
            dst_ref=recv.at[2 - o, t],
            send_sem=send_sem.at[o, i],
            recv_sem=recv_sem.at[o, i],
            device_id=target,
            device_id_type=MESH,
        )
        copy.start()
        sends.append(copy)

    wi[pl.ds(wi_hbm.shape[0], wi.shape[0] - wi_hbm.shape[0])] = jnp.zeros(
        (wi.shape[0] - wi_hbm.shape[0], wide), jnp.bfloat16
    )

    @pl.loop(0, chunks)
    def _(i):
        pltpu.make_async_copy(
            wt_hbm.at[pl.ds(i * CHUNK, CHUNK)], raw.at[i], raw_sem.at[i]
        ).wait()
        for h in range(CHUNK // 16):
            piece = jnp.swapaxes(raw[i, h * 16 : h * 16 + 16], 0, 1)
            place_at = pl.multiple_of(i * CHUNK + h * 16, 16)
            for tap in range(2 * stride):
                if half <= tap < half + stride:
                    table[tap - half, pl.ds(place_at, 16)] = piece[tap]
                else:
                    phase = (tap + half) % stride if tap < half else tap - stride - half
                    table[phase, pl.ds(wide + place_at, 16)] = piece[tap]

    own.wait()
    for copy in sends:
        copy.wait()
    wi_copy.wait()

    lens = (lens_ref[0], lens_ref[1])
    lane = lax.broadcasted_iota(jnp.int32, (1, 128), 1)
    edge = (128 - frames) // 2
    for track in range(2):
        def slab(o):
            piece = recv[o, :, track].reshape(track_count * part, frames).astype(jnp.float32)
            return jnp.concatenate(
                [piece, jnp.zeros((track_count * part, 128 - frames), jnp.float32)], axis=1
            )

        low = pltpu.roll(slab(0), 128 + edge - frames, 1)
        mid = pltpu.roll(slab(1), edge, 1)
        high = pltpu.roll(slab(2), edge + frames, 1)
        joined = jnp.where(lane < edge, low, jnp.where(lane < edge + frames, mid, high))
        place_of = base + lane - edge
        joined = jnp.where((place_of >= 0) & (place_of < lens[track]), joined, 0.0)
        stacked = [
            pltpu.roll(joined, 128 - (k - taps // 2 + edge - LEAD), 1) for k in range(taps)
        ]
        missing = wi.shape[0] - taps * track_count * part
        stacked.append(jnp.zeros((missing, 128), jnp.float32))
        block = jnp.concatenate(stacked, axis=0).T
        columns[pl.ds(track * per_track, per_track)] = block[:per_track]

    row = lax.broadcasted_iota(jnp.int32, (rows, 1), 0)
    live = live_rows(row, per_track, base, LEAD, lens)
    lhs = columns[...].astype(jnp.bfloat16)
    for n in range(0, wide, 256):
        hidden = jnp.dot(lhs, wi[:, n : n + 256], preferred_element_type=jnp.float32)
        hidden = jnp.where(live, hidden, 0.0).astype(jnp.bfloat16).astype(jnp.float32)
        turn = up_ref[0:1, n : n + 256] * (1.0 / math.pi)
        value = snake(hidden, turn, 1.0 / up_ref[1:2, n : n + 256])
        plain = value.astype(jnp.bfloat16)
        shaped[0, :, n : n + 256] = plain
        shaped[1, :, n : n + 256] = plain
        shaped[0, :, wide + n : wide + n + 256] = pltpu.roll(value, 1, 0).astype(jnp.bfloat16)
        shaped[1, :, wide + n : wide + n + 256] = pltpu.roll(value, rows - 1, 0).astype(jnp.bfloat16)

    def coefficients(u, i):
        return res_ref[u, i, 0:1] * (1.0 / math.pi), 1.0 / res_ref[u, i, 1:2]

    first = coefficients(0, 0)

    @pl.loop(0, stride)
    def _(p):
        summed = jnp.dot(shaped[p // half], table[p], preferred_element_type=jnp.float32)
        signal = jnp.where(live, summed, 0.0).astype(jnp.bfloat16)
        sig0[p] = signal
        value = snake(signal.astype(jnp.float32), *first)
        act0[p + 3] = value.astype(jnp.bfloat16)

        @pl.when(p <= 2)
        def _():
            act0[p + 11] = pltpu.roll(value, rows - 1, 0).astype(jnp.bfloat16)

        @pl.when(p >= stride - 3)
        def _():
            act0[p - 5] = pltpu.roll(value, 1, 0).astype(jnp.bfloat16)

    wd_copies[0].wait()
    wp_copy.wait()
    second = coefficients(0, 1)
    third = coefficients(1, 0)

    def inner(value, shift):
        moved = pltpu.roll(value, rows - (LEAD + shift), 0)
        return jnp.concatenate([moved[:frames], moved[per_track : per_track + frames]], axis=0)

    @pl.loop(0, stride // GROUP)
    def _(step):
        p0 = step * GROUP
        summed = jnp.zeros((GROUP * rows, width), jnp.float32)
        for k in range(taps):
            window = act0[pl.ds(p0 + k, GROUP)].reshape(GROUP * rows, width)
            summed = summed + jnp.dot(window, wd[0, k], preferred_element_type=jnp.float32)
        pointed = snake(summed, *second).astype(jnp.bfloat16)
        branch = jnp.dot(pointed, wp[0], preferred_element_type=jnp.float32)
        for j in range(GROUP):
            p = p0 + j
            total = sig0[p].astype(jnp.float32) + branch[j * rows : (j + 1) * rows]
            signal = jnp.where(live, total, 0.0).astype(jnp.bfloat16).astype(jnp.float32)
            sig1[p] = inner(signal, 0).astype(jnp.bfloat16)
            value = snake(signal, *third)
            act1[p + 9] = inner(value, 0).astype(jnp.bfloat16)
            act1[p + 17] = inner(value, 1).astype(jnp.bfloat16)
            act1[p + 1] = inner(value, -1).astype(jnp.bfloat16)

            @pl.when(p == 0)
            def _():
                act1[25] = inner(value, 2).astype(jnp.bfloat16)

            @pl.when(p == stride - 1)
            def _():
                act1[0] = inner(value, -2).astype(jnp.bfloat16)

    wd_copies[1].wait()
    fourth = coefficients(1, 1)
    core = 2 * frames
    core_row = lax.broadcasted_iota(jnp.int32, (core, 1), 0)
    core_live = live_rows(core_row, frames, base, 0, lens)

    @pl.loop(0, stride // GROUP)
    def _(step):
        p0 = step * GROUP
        summed = jnp.zeros((GROUP * core, width), jnp.float32)
        for k in range(taps):
            window = act1[pl.ds(p0 + 3 * k, GROUP)].reshape(GROUP * core, width)
            summed = summed + jnp.dot(window, wd[1, k], preferred_element_type=jnp.float32)
        pointed = snake(summed, *fourth).astype(jnp.bfloat16)
        branch = jnp.dot(pointed, wp[1], preferred_element_type=jnp.float32)
        for j in range(GROUP):
            total = sig1[p0 + j].astype(jnp.float32) + branch[j * core : (j + 1) * core]
            final[p0 + j] = jnp.where(core_live, total, 0.0)

    for track in range(2):
        for c in range(frames // 16):
            block = jnp.swapaxes(final[:, track * frames + c * 16 : track * frames + c * 16 + 16], 0, 1)
            out_ref[track, c * 16 * stride : (c + 1) * 16 * stride] = block.reshape(
                16 * stride, width
            ).astype(jnp.bfloat16)


def local(mesh, latents, lengths, w_in, up_params, w_up, res_params, w_dil, w_point):
    track_count, time_count = mesh.shape["track"], mesh.shape["tm"]
    part_tracks, frames, part = latents.shape[0] // track_count, latents.shape[1], latents.shape[2]
    taps, _, wide = w_in.shape
    stride, width = w_up.shape[1] // 2, w_up.shape[2]
    rows = 2 * (frames + 2 * LEAD)
    depth = -(-taps * track_count * part // 128) * 128
    chunks = wide // CHUNK
    bf = jnp.bfloat16
    vmem = pl.BlockSpec(memory_space=pltpu.VMEM)
    hbm = pl.BlockSpec(memory_space=pl.ANY)
    return pl.pallas_call(
        functools.partial(kernel, track_count, time_count),
        out_shape=jax.ShapeDtypeStruct((part_tracks, frames * stride, width), bf),
        in_specs=[pl.BlockSpec(memory_space=pltpu.SMEM), vmem, vmem, vmem, hbm, hbm, hbm, hbm],
        out_specs=vmem,
        scratch_shapes=[
            pltpu.VMEM((3, track_count, 2, part, frames), bf),
            pltpu.VMEM((depth, wide), bf),
            pltpu.VMEM((chunks, CHUNK, 2 * stride, width), bf),
            pltpu.VMEM((stride, 2 * wide, width), bf),
            pltpu.VMEM(w_dil.shape, bf),
            pltpu.VMEM(w_point.shape, bf),
            pltpu.VMEM((rows, depth), jnp.float32),
            pltpu.VMEM((2, rows, 2 * wide), bf),
            pltpu.VMEM((stride, rows, width), bf),
            pltpu.VMEM((stride, 2 * frames, width), bf),
            pltpu.VMEM((stride + 6, rows, width), bf),
            pltpu.VMEM((stride + 18, 2 * frames, width), bf),
            pltpu.VMEM((stride, 2 * frames, width), jnp.float32),
            pltpu.SemaphoreType.DMA((3, track_count)),
            pltpu.SemaphoreType.DMA((3, track_count)),
            pltpu.SemaphoreType.DMA,
            pltpu.SemaphoreType.DMA,
            pltpu.SemaphoreType.DMA((chunks,)),
            pltpu.SemaphoreType.DMA((2,)),
            pltpu.SemaphoreType.DMA,
        ],
        compiler_params=pltpu.CompilerParams(
            collective_id=0, has_side_effects=True, vmem_limit_bytes=63 * 2**20
        ),
        name="decoder",
    )(
        lengths,
        jnp.transpose(latents, (0, 2, 1)),
        up_params,
        res_params,
        w_in.reshape(taps * w_in.shape[1], wide),
        w_up,
        w_dil,
        w_point,
    )


def solution(mesh):
    in_specs = (P(None, "tm", "track"), P("track"), P(), P(), P(), P(), P(), P())
    out_specs = P("track", "tm", None)
    return jax.shard_map(
        functools.partial(local, mesh),
        mesh=mesh,
        in_specs=in_specs,
        out_specs=out_specs,
        check_vma=False,
    )
```

```python
import functools
import math

import jax
import jax.numpy as jnp
from jax import lax
from jax.experimental import pallas as pl
from jax.experimental.pallas import tpu as pltpu
from jax.sharding import PartitionSpec as P

MESH = pl.DeviceIdType.MESH
LEAD = 4
CHUNK = 64
GROUP = 2
SIN2 = (9.86952174, -32.4650355, 42.6422709, -29.4210797, 10.573119)


def snake(value, turn, gain):
    turns = value * turn
    rest = turns - jnp.round(turns)
    square = rest * rest
    wave = SIN2[-1]
    for factor in SIN2[-2::-1]:
        wave = wave * square + factor
    return value + (wave * square) * gain


def live_rows(row, per_track, base, lead, lens):
    second = row >= per_track
    frame = base - lead + row - jnp.where(second, per_track, 0)
    limit = jnp.where(second, lens[1], lens[0])
    return (frame >= 0) & (frame < limit)


def kernel(
    track_count,
    time_count,
    lens_ref,
    x_ref,
    up_ref,
    res_ref,
    wi_hbm,
    wt_hbm,
    wd_hbm,
    wp_hbm,
    out_ref,
    recv,
    wi,
    raw,
    table,
    wd,
    wp,
    columns,
    shaped,
    sig0,
    sig1,
    act0,
    act1,
    final,
    send_sem,
    recv_sem,
    own_sem,
    wi_sem,
    raw_sem,
    wd_sem,
    wp_sem,
):
    frames = x_ref.shape[2]
    rows = shaped.shape[1]
    per_track = rows // 2
    stride = sig0.shape[0]
    half = stride // 2
    width = sig0.shape[2]
    wide = table.shape[1] // 2
    part = x_ref.shape[1]
    taps = wd.shape[1]
    t = lax.axis_index("track")
    m = lax.axis_index("tm")
    base = m * frames

    chunks = raw.shape[0]
    wi_copy = pltpu.make_async_copy(wi_hbm, wi.at[pl.ds(0, wi_hbm.shape[0])], wi_sem)
    wi_copy.start()
    raw_copies = [
        pltpu.make_async_copy(wt_hbm.at[pl.ds(i * CHUNK, CHUNK)], raw.at[i], raw_sem.at[i])
        for i in range(chunks)
    ]
    for copy in raw_copies:
        copy.start()
    wd_copies = [pltpu.make_async_copy(wd_hbm.at[u], wd.at[u], wd_sem.at[u]) for u in range(2)]
    wp_copy = pltpu.make_async_copy(wp_hbm, wp, wp_sem)
    wd_copies[0].start()
    wp_copy.start()
    wd_copies[1].start()

    peers = []
    for o in range(3):
        for i in range(track_count):
            if o == 1 and i == 0:
                continue
            peers.append((o, i))
    barrier = pltpu.get_barrier_semaphore()

    def place(o, i):
        return {
            "track": lax.rem(t + i, track_count),
            "tm": m + o - 1,
        }

    inside = {0: m > 0, 1: None, 2: m < time_count - 1}

    def guarded(o, action):
        if inside[o] is None:
            action()
        else:
            pl.when(inside[o])(action)

    def greet(o, i):
        pl.semaphore_signal(barrier, inc=1, device_id=place(o, i), device_id_type=MESH)

    for o, i in peers:
        guarded(o, functools.partial(greet, o, i))
    sides = jnp.where(m > 0, 1, 0) + jnp.where(m < time_count - 1, 1, 0)
    pl.semaphore_wait(barrier, track_count - 1 + track_count * sides)
    own = pltpu.make_async_copy(x_ref.at[pl.ds(2 * t, 2)], recv.at[1, t], own_sem)
    own.start()
    sends = []
    for o, i in peers:
        target = place(o, i)
        copy = pltpu.make_async_remote_copy(
            src_ref=x_ref.at[pl.ds(2 * target["track"], 2)],
            dst_ref=recv.at[2 - o, t],
            send_sem=send_sem.at[o, i],
            recv_sem=recv_sem.at[o, i],
            device_id=target,
            device_id_type=MESH,
        )
        guarded(o, copy.start)
        sends.append((o, copy))

    wi[pl.ds(wi_hbm.shape[0], wi.shape[0] - wi_hbm.shape[0])] = jnp.zeros(
        (wi.shape[0] - wi_hbm.shape[0], wide), jnp.bfloat16
    )

    @pl.loop(0, chunks)
    def _(i):
        pltpu.make_async_copy(
            wt_hbm.at[pl.ds(i * CHUNK, CHUNK)], raw.at[i], raw_sem.at[i]
        ).wait()
        for h in range(CHUNK // 16):
            piece = jnp.swapaxes(raw[i, h * 16 : h * 16 + 16], 0, 1)
            place_at = pl.multiple_of(i * CHUNK + h * 16, 16)
            for tap in range(2 * stride):
                if half <= tap < half + stride:
                    table[tap - half, pl.ds(place_at, 16)] = piece[tap]
                else:
                    phase = (tap + half) % stride if tap < half else tap - stride - half
                    table[phase, pl.ds(wide + place_at, 16)] = piece[tap]

    own.wait()
    for o, copy in sends:
        guarded(o, copy.wait_send)
        guarded(2 - o, copy.wait_recv)
    wi_copy.wait()

    lens = (lens_ref[0], lens_ref[1])
    lane = lax.broadcasted_iota(jnp.int32, (1, 128), 1)
    edge = (128 - frames) // 2
    for track in range(2):
        def slab(o):
            piece = recv[o, :, track].reshape(track_count * part, frames).astype(jnp.float32)
            return jnp.concatenate(
                [piece, jnp.zeros((track_count * part, 128 - frames), jnp.float32)], axis=1
            )

        low = pltpu.roll(slab(0), 128 + edge - frames, 1)
        mid = pltpu.roll(slab(1), edge, 1)
        high = pltpu.roll(slab(2), edge + frames, 1)
        joined = jnp.where(lane < edge, low, jnp.where(lane < edge + frames, mid, high))
        place_of = base + lane - edge
        joined = jnp.where((place_of >= 0) & (place_of < lens[track]), joined, 0.0)
        stacked = [
            pltpu.roll(joined, 128 - (k - taps // 2 + edge - LEAD), 1) for k in range(taps)
        ]
        missing = wi.shape[0] - taps * track_count * part
        stacked.append(jnp.zeros((missing, 128), jnp.float32))
        block = jnp.concatenate(stacked, axis=0).T
        columns[pl.ds(track * per_track, per_track)] = block[:per_track]

    row = lax.broadcasted_iota(jnp.int32, (rows, 1), 0)
    live = live_rows(row, per_track, base, LEAD, lens)
    lhs = columns[...].astype(jnp.bfloat16)
    for n in range(0, wide, 256):
        hidden = jnp.dot(lhs, wi[:, n : n + 256], preferred_element_type=jnp.float32)
        hidden = jnp.where(live, hidden, 0.0).astype(jnp.bfloat16).astype(jnp.float32)
        turn = up_ref[0:1, n : n + 256] * (1.0 / math.pi)
        value = snake(hidden, turn, 1.0 / up_ref[1:2, n : n + 256])
        plain = value.astype(jnp.bfloat16)
        shaped[0, :, n : n + 256] = plain
        shaped[1, :, n : n + 256] = plain
        shaped[0, :, wide + n : wide + n + 256] = pltpu.roll(value, 1, 0).astype(jnp.bfloat16)
        shaped[1, :, wide + n : wide + n + 256] = pltpu.roll(value, rows - 1, 0).astype(jnp.bfloat16)

    def coefficients(u, i):
        return res_ref[u, i, 0:1] * (1.0 / math.pi), 1.0 / res_ref[u, i, 1:2]

    first = coefficients(0, 0)

    @pl.loop(0, stride)
    def _(p):
        summed = jnp.dot(shaped[p // half], table[p], preferred_element_type=jnp.float32)
        signal = jnp.where(live, summed, 0.0).astype(jnp.bfloat16)
        sig0[p] = signal
        value = snake(signal.astype(jnp.float32), *first)
        act0[p + 3] = value.astype(jnp.bfloat16)

        @pl.when(p <= 2)
        def _():
            act0[p + 11] = pltpu.roll(value, rows - 1, 0).astype(jnp.bfloat16)

        @pl.when(p >= stride - 3)
        def _():
            act0[p - 5] = pltpu.roll(value, 1, 0).astype(jnp.bfloat16)

    wd_copies[0].wait()
    wp_copy.wait()
    second = coefficients(0, 1)
    third = coefficients(1, 0)

    def inner(value, shift):
        moved = pltpu.roll(value, rows - (LEAD + shift), 0)
        return jnp.concatenate([moved[:frames], moved[per_track : per_track + frames]], axis=0)

    @pl.loop(0, stride // GROUP)
    def _(step):
        p0 = step * GROUP
        summed = jnp.zeros((GROUP * rows, width), jnp.float32)
        for k in range(taps):
            window = act0[pl.ds(p0 + k, GROUP)].reshape(GROUP * rows, width)
            summed = summed + jnp.dot(window, wd[0, k], preferred_element_type=jnp.float32)
        pointed = snake(summed, *second).astype(jnp.bfloat16)
        branch = jnp.dot(pointed, wp[0], preferred_element_type=jnp.float32)
        for j in range(GROUP):
            p = p0 + j
            total = sig0[p].astype(jnp.float32) + branch[j * rows : (j + 1) * rows]
            signal = jnp.where(live, total, 0.0).astype(jnp.bfloat16).astype(jnp.float32)
            sig1[p] = inner(signal, 0).astype(jnp.bfloat16)
            value = snake(signal, *third)
            act1[p + 9] = inner(value, 0).astype(jnp.bfloat16)
            act1[p + 17] = inner(value, 1).astype(jnp.bfloat16)
            act1[p + 1] = inner(value, -1).astype(jnp.bfloat16)

            @pl.when(p == 0)
            def _():
                act1[25] = inner(value, 2).astype(jnp.bfloat16)

            @pl.when(p == stride - 1)
            def _():
                act1[0] = inner(value, -2).astype(jnp.bfloat16)

    wd_copies[1].wait()
    fourth = coefficients(1, 1)
    core = 2 * frames
    core_row = lax.broadcasted_iota(jnp.int32, (core, 1), 0)
    core_live = live_rows(core_row, frames, base, 0, lens)

    @pl.loop(0, stride // GROUP)
    def _(step):
        p0 = step * GROUP
        summed = jnp.zeros((GROUP * core, width), jnp.float32)
        for k in range(taps):
            window = act1[pl.ds(p0 + 3 * k, GROUP)].reshape(GROUP * core, width)
            summed = summed + jnp.dot(window, wd[1, k], preferred_element_type=jnp.float32)
        pointed = snake(summed, *fourth).astype(jnp.bfloat16)
        branch = jnp.dot(pointed, wp[1], preferred_element_type=jnp.float32)
        for j in range(GROUP):
            total = sig1[p0 + j].astype(jnp.float32) + branch[j * core : (j + 1) * core]
            final[p0 + j] = jnp.where(core_live, total, 0.0)

    for track in range(2):
        for c in range(frames // 16):
            block = jnp.swapaxes(final[:, track * frames + c * 16 : track * frames + c * 16 + 16], 0, 1)
            out_ref[track, c * 16 * stride : (c + 1) * 16 * stride] = block.reshape(
                16 * stride, width
            ).astype(jnp.bfloat16)


def local(mesh, latents, lengths, w_in, up_params, w_up, res_params, w_dil, w_point):
    track_count, time_count = mesh.shape["track"], mesh.shape["tm"]
    part_tracks, frames, part = latents.shape[0] // track_count, latents.shape[1], latents.shape[2]
    taps, _, wide = w_in.shape
    stride, width = w_up.shape[1] // 2, w_up.shape[2]
    rows = 2 * (frames + 2 * LEAD)
    depth = -(-taps * track_count * part // 128) * 128
    chunks = wide // CHUNK
    bf = jnp.bfloat16
    vmem = pl.BlockSpec(memory_space=pltpu.VMEM)
    hbm = pl.BlockSpec(memory_space=pl.ANY)
    return pl.pallas_call(
        functools.partial(kernel, track_count, time_count),
        out_shape=jax.ShapeDtypeStruct((part_tracks, frames * stride, width), bf),
        in_specs=[pl.BlockSpec(memory_space=pltpu.SMEM), vmem, vmem, vmem, hbm, hbm, hbm, hbm],
        out_specs=vmem,
        scratch_shapes=[
            pltpu.VMEM((3, track_count, 2, part, frames), bf),
            pltpu.VMEM((depth, wide), bf),
            pltpu.VMEM((chunks, CHUNK, 2 * stride, width), bf),
            pltpu.VMEM((stride, 2 * wide, width), bf),
            pltpu.VMEM(w_dil.shape, bf),
            pltpu.VMEM(w_point.shape, bf),
            pltpu.VMEM((rows, depth), jnp.float32),
            pltpu.VMEM((2, rows, 2 * wide), bf),
            pltpu.VMEM((stride, rows, width), bf),
            pltpu.VMEM((stride, 2 * frames, width), bf),
            pltpu.VMEM((stride + 6, rows, width), bf),
            pltpu.VMEM((stride + 18, 2 * frames, width), bf),
            pltpu.VMEM((stride, 2 * frames, width), jnp.float32),
            pltpu.SemaphoreType.DMA((3, track_count)),
            pltpu.SemaphoreType.DMA((3, track_count)),
            pltpu.SemaphoreType.DMA,
            pltpu.SemaphoreType.DMA,
            pltpu.SemaphoreType.DMA((chunks,)),
            pltpu.SemaphoreType.DMA((2,)),
            pltpu.SemaphoreType.DMA,
        ],
        compiler_params=pltpu.CompilerParams(
            collective_id=0, has_side_effects=True, vmem_limit_bytes=63 * 2**20
        ),
        name="decoder",
    )(
        lengths,
        jnp.transpose(latents, (0, 2, 1)),
        up_params,
        res_params,
        w_in.reshape(taps * w_in.shape[1], wide),
        w_up,
        w_dil,
        w_point,
    )


def solution(mesh):
    in_specs = (P(None, "tm", "track"), P("track"), P(), P(), P(), P(), P(), P())
    out_specs = P("track", "tm", None)
    return jax.shard_map(
        functools.partial(local, mesh),
        mesh=mesh,
        in_specs=in_specs,
        out_specs=out_specs,
        check_vma=False,
    )
```

```python
import functools
import math

import jax
import jax.numpy as jnp
from jax import lax
from jax.experimental import pallas as pl
from jax.experimental.pallas import tpu as pltpu
from jax.sharding import PartitionSpec as P

MESH = pl.DeviceIdType.MESH
LEAD = 4
CHUNK = 64
GROUP = 2
SIN2 = (9.86952174, -32.4650355, 42.6422709, -29.4210797, 10.573119)


def snake(value, turn, gain):
    turns = value * turn
    rest = turns - jnp.round(turns)
    square = rest * rest
    wave = SIN2[-1]
    for factor in SIN2[-2::-1]:
        wave = wave * square + factor
    return value + (wave * square) * gain


def live_rows(row, per_track, base, lead, lens):
    second = row >= per_track
    frame = base - lead + row - jnp.where(second, per_track, 0)
    limit = jnp.where(second, lens[1], lens[0])
    return (frame >= 0) & (frame < limit)


def kernel(
    track_count,
    time_count,
    lens_ref,
    x_ref,
    up_ref,
    res_ref,
    wi_hbm,
    wt_hbm,
    wd_hbm,
    wp_hbm,
    out_ref,
    recv,
    wi,
    raw,
    table,
    wd,
    wp,
    columns,
    shaped,
    sig0,
    sig1,
    act0,
    act1,
    final,
    send_sem,
    recv_sem,
    own_sem,
    wi_sem,
    raw_sem,
    wd_sem,
    wp_sem,
):
    frames = x_ref.shape[2]
    rows = shaped.shape[1]
    per_track = rows // 2
    stride = sig0.shape[0]
    half = stride // 2
    width = sig0.shape[2]
    wide = table.shape[1] // 2
    part = x_ref.shape[1]
    taps = wd.shape[1]
    t = lax.axis_index("track")
    m = lax.axis_index("tm")
    base = m * frames

    chunks = raw.shape[0]
    wi_copy = pltpu.make_async_copy(wi_hbm, wi.at[pl.ds(0, wi_hbm.shape[0])], wi_sem)
    wi_copy.start()
    raw_copies = [
        pltpu.make_async_copy(wt_hbm.at[pl.ds(i * CHUNK, CHUNK)], raw.at[i], raw_sem.at[i])
        for i in range(chunks)
    ]
    for copy in raw_copies:
        copy.start()
    wd_copies = [pltpu.make_async_copy(wd_hbm.at[u], wd.at[u], wd_sem.at[u]) for u in range(2)]
    wp_copy = pltpu.make_async_copy(wp_hbm, wp, wp_sem)
    wd_copies[0].start()
    wp_copy.start()
    wd_copies[1].start()

    peers = []
    for o in range(3):
        for i in range(track_count):
            if o == 1 and i == 0:
                continue
            peers.append((o, i))
    barrier = pltpu.get_barrier_semaphore()

    def place(o, i):
        return {
            "track": lax.rem(t + i, track_count),
            "tm": m + o - 1,
        }

    inside = {0: m > 0, 1: None, 2: m < time_count - 1}

    def guarded(o, action):
        if inside[o] is None:
            action()
        else:
            pl.when(inside[o])(action)

    def greet(o, i):
        pl.semaphore_signal(barrier, inc=1, device_id=place(o, i), device_id_type=MESH)

    for o, i in peers:
        guarded(o, functools.partial(greet, o, i))
    sides = jnp.where(m > 0, 1, 0) + jnp.where(m < time_count - 1, 1, 0)
    pl.semaphore_wait(barrier, track_count - 1 + track_count * sides)
    own = pltpu.make_async_copy(x_ref.at[pl.ds(2 * t, 2)], recv.at[1, t], own_sem)
    own.start()
    sends = []
    for o, i in peers:
        target = place(o, i)
        copy = pltpu.make_async_remote_copy(
            src_ref=x_ref.at[pl.ds(2 * target["track"], 2)],
            dst_ref=recv.at[2 - o, t],
            send_sem=send_sem.at[o, i],
            recv_sem=recv_sem.at[o, i],
            device_id=target,
            device_id_type=MESH,
        )
        guarded(o, copy.start)
        sends.append((o, copy))

    wi[pl.ds(wi_hbm.shape[0], wi.shape[0] - wi_hbm.shape[0])] = jnp.zeros(
        (wi.shape[0] - wi_hbm.shape[0], wide), jnp.bfloat16
    )

    @pl.loop(0, chunks)
    def _(i):
        pltpu.make_async_copy(
            wt_hbm.at[pl.ds(i * CHUNK, CHUNK)], raw.at[i], raw_sem.at[i]
        ).wait()
        for h in range(CHUNK // 16):
            piece = jnp.swapaxes(raw[i, h * 16 : h * 16 + 16], 0, 1)
            place_at = pl.multiple_of(i * CHUNK + h * 16, 16)
            for tap in range(2 * stride):
                if half <= tap < half + stride:
                    table[tap - half, pl.ds(place_at, 16)] = piece[tap]
                else:
                    phase = (tap + half) % stride if tap < half else tap - stride - half
                    table[phase, pl.ds(wide + place_at, 16)] = piece[tap]

    own.wait()
    for o, copy in sends:
        guarded(o, copy.wait_send)
        guarded(2 - o, copy.wait_recv)
    wi_copy.wait()

    lens = (lens_ref[0], lens_ref[1])
    lane = lax.broadcasted_iota(jnp.int32, (1, 128), 1)
    edge = (128 - frames) // 2
    for track in range(2):
        def slab(o):
            piece = recv[o, :, track].reshape(track_count * part, frames).astype(jnp.float32)
            return jnp.concatenate(
                [piece, jnp.zeros((track_count * part, 128 - frames), jnp.float32)], axis=1
            )

        low = pltpu.roll(slab(0), 128 + edge - frames, 1)
        mid = pltpu.roll(slab(1), edge, 1)
        high = pltpu.roll(slab(2), edge + frames, 1)
        joined = jnp.where(lane < edge, low, jnp.where(lane < edge + frames, mid, high))
        place_of = base + lane - edge
        joined = jnp.where((place_of >= 0) & (place_of < lens[track]), joined, 0.0)
        stacked = [
            pltpu.roll(joined, 128 - (k - taps // 2 + edge - LEAD), 1) for k in range(taps)
        ]
        missing = wi.shape[0] - taps * track_count * part
        stacked.append(jnp.zeros((missing, 128), jnp.float32))
        block = jnp.concatenate(stacked, axis=0).T
        columns[pl.ds(track * per_track, per_track)] = block[:per_track]

    row = lax.broadcasted_iota(jnp.int32, (rows, 1), 0)
    live = live_rows(row, per_track, base, LEAD, lens)
    lhs = columns[...].astype(jnp.bfloat16)
    for n in range(0, wide, 256):
        hidden = jnp.dot(lhs, wi[:, n : n + 256], preferred_element_type=jnp.float32)
        hidden = jnp.where(live, hidden, 0.0).astype(jnp.bfloat16).astype(jnp.float32)
        turn = up_ref[0:1, n : n + 256] * (1.0 / math.pi)
        value = snake(hidden, turn, 1.0 / up_ref[1:2, n : n + 256])
        plain = value.astype(jnp.bfloat16)
        shaped[0, :, n : n + 256] = plain
        shaped[1, :, n : n + 256] = plain
        shaped[0, :, wide + n : wide + n + 256] = pltpu.roll(value, 1, 0).astype(jnp.bfloat16)
        shaped[1, :, wide + n : wide + n + 256] = pltpu.roll(value, rows - 1, 0).astype(jnp.bfloat16)

    def coefficients(u, i):
        return res_ref[u, i, 0:1] * (1.0 / math.pi), 1.0 / res_ref[u, i, 1:2]

    first = coefficients(0, 0)

    @pl.loop(0, stride, unroll=True)
    def _(p):
        summed = jnp.dot(shaped[p // half], table[p], preferred_element_type=jnp.float32)
        signal = jnp.where(live, summed, 0.0).astype(jnp.bfloat16)
        sig0[p] = signal
        value = snake(signal.astype(jnp.float32), *first)
        act0[p + 3] = value.astype(jnp.bfloat16)

        @pl.when(p <= 2)
        def _():
            act0[p + 11] = pltpu.roll(value, rows - 1, 0).astype(jnp.bfloat16)

        @pl.when(p >= stride - 3)
        def _():
            act0[p - 5] = pltpu.roll(value, 1, 0).astype(jnp.bfloat16)

    wd_copies[0].wait()
    wp_copy.wait()
    second = coefficients(0, 1)
    third = coefficients(1, 0)

    def inner(value, shift):
        moved = pltpu.roll(value, rows - (LEAD + shift), 0)
        return jnp.concatenate([moved[:frames], moved[per_track : per_track + frames]], axis=0)

    @pl.loop(0, stride // GROUP, unroll=True)
    def _(step):
        p0 = step * GROUP
        summed = jnp.zeros((GROUP * rows, width), jnp.float32)
        for k in range(taps):
            window = act0[pl.ds(p0 + k, GROUP)].reshape(GROUP * rows, width)
            summed = summed + jnp.dot(window, wd[0, k], preferred_element_type=jnp.float32)
        pointed = snake(summed, *second).astype(jnp.bfloat16)
        branch = jnp.dot(pointed, wp[0], preferred_element_type=jnp.float32)
        for j in range(GROUP):
            p = p0 + j
            total = sig0[p].astype(jnp.float32) + branch[j * rows : (j + 1) * rows]
            signal = jnp.where(live, total, 0.0).astype(jnp.bfloat16).astype(jnp.float32)
            sig1[p] = inner(signal, 0).astype(jnp.bfloat16)
            value = snake(signal, *third)
            act1[p + 9] = inner(value, 0).astype(jnp.bfloat16)
            act1[p + 17] = inner(value, 1).astype(jnp.bfloat16)
            act1[p + 1] = inner(value, -1).astype(jnp.bfloat16)

            @pl.when(p == 0)
            def _():
                act1[25] = inner(value, 2).astype(jnp.bfloat16)

            @pl.when(p == stride - 1)
            def _():
                act1[0] = inner(value, -2).astype(jnp.bfloat16)

    wd_copies[1].wait()
    fourth = coefficients(1, 1)
    core = 2 * frames
    core_row = lax.broadcasted_iota(jnp.int32, (core, 1), 0)
    core_live = live_rows(core_row, frames, base, 0, lens)

    @pl.loop(0, stride // GROUP, unroll=True)
    def _(step):
        p0 = step * GROUP
        summed = jnp.zeros((GROUP * core, width), jnp.float32)
        for k in range(taps):
            window = act1[pl.ds(p0 + 3 * k, GROUP)].reshape(GROUP * core, width)
            summed = summed + jnp.dot(window, wd[1, k], preferred_element_type=jnp.float32)
        pointed = snake(summed, *fourth).astype(jnp.bfloat16)
        branch = jnp.dot(pointed, wp[1], preferred_element_type=jnp.float32)
        for j in range(GROUP):
            total = sig1[p0 + j].astype(jnp.float32) + branch[j * core : (j + 1) * core]
            final[p0 + j] = jnp.where(core_live, total, 0.0)

    for track in range(2):
        for c in range(frames // 16):
            block = jnp.swapaxes(final[:, track * frames + c * 16 : track * frames + c * 16 + 16], 0, 1)
            out_ref[track, c * 16 * stride : (c + 1) * 16 * stride] = block.reshape(
                16 * stride, width
            ).astype(jnp.bfloat16)


def local(mesh, latents, lengths, w_in, up_params, w_up, res_params, w_dil, w_point):
    track_count, time_count = mesh.shape["track"], mesh.shape["tm"]
    part_tracks, frames, part = latents.shape[0] // track_count, latents.shape[1], latents.shape[2]
    taps, _, wide = w_in.shape
    stride, width = w_up.shape[1] // 2, w_up.shape[2]
    rows = 2 * (frames + 2 * LEAD)
    depth = -(-taps * track_count * part // 128) * 128
    chunks = wide // CHUNK
    bf = jnp.bfloat16
    vmem = pl.BlockSpec(memory_space=pltpu.VMEM)
    hbm = pl.BlockSpec(memory_space=pl.ANY)
    return pl.pallas_call(
        functools.partial(kernel, track_count, time_count),
        out_shape=jax.ShapeDtypeStruct((part_tracks, frames * stride, width), bf),
        in_specs=[pl.BlockSpec(memory_space=pltpu.SMEM), vmem, vmem, vmem, hbm, hbm, hbm, hbm],
        out_specs=vmem,
        scratch_shapes=[
            pltpu.VMEM((3, track_count, 2, part, frames), bf),
            pltpu.VMEM((depth, wide), bf),
            pltpu.VMEM((chunks, CHUNK, 2 * stride, width), bf),
            pltpu.VMEM((stride, 2 * wide, width), bf),
            pltpu.VMEM(w_dil.shape, bf),
            pltpu.VMEM(w_point.shape, bf),
            pltpu.VMEM((rows, depth), jnp.float32),
            pltpu.VMEM((2, rows, 2 * wide), bf),
            pltpu.VMEM((stride, rows, width), bf),
            pltpu.VMEM((stride, 2 * frames, width), bf),
            pltpu.VMEM((stride + 6, rows, width), bf),
            pltpu.VMEM((stride + 18, 2 * frames, width), bf),
            pltpu.VMEM((stride, 2 * frames, width), jnp.float32),
            pltpu.SemaphoreType.DMA((3, track_count)),
            pltpu.SemaphoreType.DMA((3, track_count)),
            pltpu.SemaphoreType.DMA,
            pltpu.SemaphoreType.DMA,
            pltpu.SemaphoreType.DMA((chunks,)),
            pltpu.SemaphoreType.DMA((2,)),
            pltpu.SemaphoreType.DMA,
        ],
        compiler_params=pltpu.CompilerParams(
            collective_id=0, has_side_effects=True, vmem_limit_bytes=63 * 2**20
        ),
        name="decoder",
    )(
        lengths,
        jnp.transpose(latents, (0, 2, 1)),
        up_params,
        res_params,
        w_in.reshape(taps * w_in.shape[1], wide),
        w_up,
        w_dil,
        w_point,
    )


def solution(mesh):
    in_specs = (P(None, "tm", "track"), P("track"), P(), P(), P(), P(), P(), P())
    out_specs = P("track", "tm", None)
    return jax.shard_map(
        functools.partial(local, mesh),
        mesh=mesh,
        in_specs=in_specs,
        out_specs=out_specs,
        check_vma=False,
    )
```
